128 devices in a mesh: dom: 128 (over x, z, y, core).
Axes of the slice: x: 4, y: 4, z: 4, core: 2. Of those that a mesh axis runs over, the one named last changes fastest.
Arguments:
- states: bfloat16 [262144, 768], P('dom'), may hold values from -6 to 6
- pre_act: bfloat16 [262144, 768], P('dom'), may hold values from -6 to 6
- features: bfloat16 [262144, 256], P('dom'), may hold values from -6 to 6
- cotangent: bfloat16 [262144, 256], P('dom'), may hold values from -6 to 6
- halo_states: bfloat16 [73728, 768], P('dom'), may hold values from -6 to 6
- halo_cot: bfloat16 [73728, 768], P('dom'), may hold values from -2 to 2
- coupling: bfloat16 [262144, 576], P('dom'), may hold values from -0.25 to 0.25
- tile_blocks: bfloat16 [8192, 128, 128], P('dom'), may hold values from -0.25 to 0.25
- tile_rows: int32 [8192], P('dom'), may hold values from 0 to 15
- tile_cols: int32 [8192], P('dom'), may hold values from 0 to 15
- tile_counts: int32 [128], P('dom'), may hold values from 16 to 64, as said below
- send_rows: int32 [1152, 64], P('dom'), may hold values from 0 to 2047
- send_counts: int32 [1152], P('dom'), may hold values from 22 to 64, as said below
- recv_counts: int32 [1152], P('dom'), may hold values from 22 to 64, as said below
- w_state: bfloat16 [3, 256, 256], replicated, may hold values from -0.375 to 0.375
- w_input: bfloat16 [3, 256, 256], replicated, may hold values from -0.375 to 0.375
Outputs:
- state_grad: bfloat16 [262144, 768], P('dom')
- feature_grad: bfloat16 [262144, 256], P('dom')
- weight_grad: float32 [3, 256, 256], replicated
- input_grad: float32 [3, 256, 256], replicated
- sent_cot: bfloat16 [73728, 768], P('dom')
The draws below stay inside these ranges and needn't reach their ends.
Inputs may be any that keep to these rules, and one draw needn't show every extreme that they name: `send_counts`: partition p sends slot j to partition (p + offset_j) mod 128; some slot of some partition holds exactly 64 rows in every draw. recv_counts[q * 9 + j] equals send_counts[p * 9 + j] for p = (q - offset_j) mod 128. `tile_counts`: some partition has all 64 slots live in every draw.
All inputs are finite; a program needn't handle non-finite values.
Results may differ from the reference program's by a relative error of at most 0.0055.
Values may be sent and summed in bfloat16 or wider, within the bound.
A program may use at most 192 MiB of HBM per device.

```python
import math
import jax
import jax.numpy as jnp
from jax import lax

C = 256
K = 3
KC = 768
TB = 128
ROWS = 2048
RBLK = 16
TILE_ROW = 4
TMAX = 64
OFFS = 9
CAP = 64
HALO = 576
NPARTS = 128
NODES = 262144


def partner_loads(key):
    grid_vals = jax.random.randint(key, (NPARTS, OFFS), (CAP + 2) // 3, CAP + 1)
    chosen = jax.random.randint(jax.random.fold_in(key, 7), (), 0, NPARTS * OFFS)
    return grid_vals.reshape(-1).at[chosen].set(CAP).reshape(NPARTS, OFFS)


def draw_send_counts(key, part):
    return partner_loads(key).reshape(-1).astype(jnp.int32)


def draw_recv_counts(key, part):
    grid_vals = partner_loads(key)
    reach = (OFFS - 1) // 2
    offsets = list(range(1, reach + 1)) + [-stride for stride in range(1, reach + 1)] + [NPARTS // 2]
    columns = [jnp.roll(grid_vals[:, slot_index], offsets[slot_index]) for slot_index in range(OFFS)]
    return jnp.stack(columns, axis=1).reshape(-1).astype(jnp.int32)


def draw_tile_counts(key, part):
    key = jax.random.fold_in(key, 11)
    counts = jax.random.randint(key, (NPARTS,), (TMAX + 3) // 4, TMAX + 1)
    chosen = jax.random.randint(jax.random.fold_in(key, 12), (), 0, NPARTS)
    return counts.at[chosen].set(TMAX).astype(jnp.int32)


def plant(values, rng, least, top_value):
    longest = values.shape.index(max(values.shape))
    spots = []
    for shift in (0, 1):
        where = [jax.random.randint(jax.random.fold_in(rng, axis), (), 0, length) for axis, length in enumerate(values.shape)]
        where[longest] = (where[longest] + shift) % values.shape[longest]
        spots.append(tuple(where))
    return values.at[spots[0]].set(least).at[spots[1]].set(top_value)


def block_scale(rng, shape, split, smallest, high):
    factor_of = 1.0
    for axis_at, blocks in split:
        steps = jax.random.uniform(jax.random.fold_in(jax.random.fold_in(rng, 6), axis_at), (blocks,), jnp.float32, smallest / len(split), high / len(split))
        factor_of = factor_of * jnp.repeat(jnp.exp(steps), shape[axis_at] // blocks).reshape((-1,) + (1,) * (len(shape) - 1 - axis_at))
    return factor_of


def bell_draw(rng, shape, deviation, limit, shards=(), kind=jnp.bfloat16):
    entries = deviation * jax.random.normal(rng, shape, jnp.float32)
    if shards:
        entries = entries * block_scale(rng, shape, shards, -0.22, 0.18)
    return jnp.clip(entries, -limit, limit).astype(kind)


def setup_inputs(seed: int = 0) -> dict:
    arg_keys = jax.random.split(jax.random.key(seed), 17)
    states = bell_draw(arg_keys[0], (NODES, KC), 1.0, 6.0, ((0, 128),))
    pre_act = bell_draw(arg_keys[1], (NODES, KC), 1.0, 6.0, ((0, 128),))
    features = bell_draw(arg_keys[2], (NODES, C), 1.0, 6.0, ((0, 128),))
    cotangent = bell_draw(arg_keys[3], (NODES, C), 1.0, 6.0, ((0, 128),))
    halo_states = bell_draw(arg_keys[4], (NPARTS * HALO, KC), 1.0, 6.0, ((0, 128),))
    halo_cot = bell_draw(arg_keys[5], (NPARTS * HALO, KC), 0.3, 2.0, ((0, 128),))
    coupling = bell_draw(arg_keys[6], (NODES, HALO), HALO ** -0.5, 0.25, ((0, 128),))
    tile_blocks = bell_draw(arg_keys[7], (NPARTS * TMAX, TB, TB), (TB * TILE_ROW) ** -0.5, 0.25, ((0, 128),))
    tile_rows = plant(jax.random.randint(arg_keys[8], (NPARTS * TMAX,), 0, RBLK), jax.random.fold_in(arg_keys[8], 1), 0, RBLK - 1).astype(jnp.int32)
    tile_cols = plant(jax.random.randint(arg_keys[9], (NPARTS * TMAX,), 0, RBLK), jax.random.fold_in(arg_keys[9], 1), 0, RBLK - 1).astype(jnp.int32)
    tile_counts = draw_tile_counts(jax.random.fold_in(arg_keys[16], 71), 0)
    send_rows = plant(jax.random.randint(arg_keys[11], (NPARTS * OFFS, CAP), 0, ROWS), jax.random.fold_in(arg_keys[11], 1), 0, ROWS - 1).astype(jnp.int32)
    send_counts = draw_send_counts(jax.random.fold_in(arg_keys[16], 71), 0)
    recv_counts = draw_recv_counts(jax.random.fold_in(arg_keys[16], 71), 0)
    w_state = bell_draw(arg_keys[14], (K, C, C), C ** -0.5, 0.375)
    w_input = bell_draw(arg_keys[15], (K, C, C), C ** -0.5, 0.375)
    return dict(states=states, pre_act=pre_act, features=features, cotangent=cotangent, halo_states=halo_states, halo_cot=halo_cot, coupling=coupling, tile_blocks=tile_blocks, tile_rows=tile_rows, tile_cols=tile_cols, tile_counts=tile_counts, send_rows=send_rows, send_counts=send_counts, recv_counts=recv_counts, w_state=w_state, w_input=w_input)


def offset_list():
    reach = (OFFS - 1) // 2
    return list(range(1, reach + 1)) + [-stride for stride in range(1, reach + 1)] + [NPARTS // 2]

def tile_apply(blocks, rows_at, cols_at, live_count, values, flipped):
    is_live = (jnp.arange(TMAX, dtype=jnp.int32) < live_count).astype(jnp.bfloat16)
    live_tiles = (blocks * is_live[:, None, None]).astype(jnp.float32)
    blocked = values.reshape(RBLK, TB, KC)
    if flipped:
        sources = blocked[rows_at].astype(jnp.float32)
        products = jnp.einsum('tli,tlc->tic', live_tiles, sources)
        targets = cols_at
    else:
        sources = blocked[cols_at].astype(jnp.float32)
        products = jnp.einsum('til,tlc->tic', live_tiles, sources)
        targets = rows_at
    summed = jax.ops.segment_sum(products, targets, num_segments=RBLK)
    return summed.reshape(ROWS, KC)

def reference(states, pre_act, features, cotangent, halo_states, halo_cot, coupling, tile_blocks, tile_rows, tile_cols, tile_counts, send_rows, send_counts, recv_counts, w_state, w_input):
    repeated = jnp.tile(cotangent.astype(jnp.float32), (1, K))
    pre_grad = (jnp.where(pre_act > 0, repeated, jnp.zeros((), jnp.float32)) / 3.0).astype(jnp.bfloat16)
    grad_parts = pre_grad.reshape(NPARTS, ROWS, KC)
    send_grid = send_rows.reshape(NPARTS, OFFS, CAP)
    counts_table = send_counts.reshape(NPARTS, OFFS)
    offsets = jnp.array(offset_list(), dtype=jnp.int32)
    anchor = (jnp.arange(NPARTS, dtype=jnp.int32)[:, None] - offsets[None, :]) % NPARTS
    slot_ids = jnp.broadcast_to(jnp.arange(OFFS, dtype=jnp.int32)[None, :], (NPARTS, OFFS))
    picked = send_grid[anchor, slot_ids]
    counts_in = counts_table[anchor, slot_ids]
    moved = grad_parts[anchor[:, :, None], picked]
    live = jnp.arange(CAP, dtype=jnp.int32)[None, None, :] < counts_in[:, :, None]
    sent_cot = jnp.where(live[..., None], moved, jnp.zeros((), jnp.bfloat16)).reshape(NPARTS * HALO, KC)

    def per_device(inputs):
        part_states, part_grad, part_feat, part_hs, part_hc, part_cp, part_tb, part_tr, part_tc, part_tn, part_rc = inputs
        col_live = (jnp.arange(CAP, dtype=jnp.int32)[None, :] < part_rc[:, None]).reshape(HALO).astype(jnp.bfloat16)
        couple_live = part_cp * col_live[None, :]
        aggregated = (tile_apply(part_tb, part_tr, part_tc, part_tn, part_states, False) + jnp.dot(couple_live, part_hs, preferred_element_type=jnp.float32)).astype(jnp.bfloat16)
        pulled = (tile_apply(part_tb, part_tr, part_tc, part_tn, part_grad, True) + jnp.dot(couple_live, part_hc, preferred_element_type=jnp.float32)).astype(jnp.bfloat16)
        grad_three = part_grad.reshape(ROWS, K, C).astype(jnp.float32)
        state_part = jnp.einsum('rkc,kdc->rkd', pulled.reshape(ROWS, K, C).astype(jnp.float32), w_state.astype(jnp.float32)).astype(jnp.bfloat16).reshape(ROWS, KC)
        feature_part = jnp.einsum('rkc,kdc->rd', grad_three, w_input.astype(jnp.float32)).astype(jnp.bfloat16)
        w_term = jnp.einsum('rkd,rkc->kdc', aggregated.reshape(ROWS, K, C).astype(jnp.float32), grad_three)
        v_term = jnp.einsum('rd,rkc->kdc', part_feat.astype(jnp.float32), grad_three)
        return (state_part, feature_part, w_term, v_term)
    inputs = (states.reshape(NPARTS, ROWS, KC), grad_parts, features.reshape(NPARTS, ROWS, C), halo_states.reshape(NPARTS, HALO, KC), halo_cot.reshape(NPARTS, HALO, KC), coupling.reshape(NPARTS, ROWS, HALO), tile_blocks.reshape(NPARTS, TMAX, TB, TB), tile_rows.reshape(NPARTS, TMAX), tile_cols.reshape(NPARTS, TMAX), tile_counts, recv_counts.reshape(NPARTS, OFFS))
    state_parts, feature_parts, w_terms, v_terms = lax.map(per_device, inputs)
    grad_scale = 1.0 / math.sqrt(NODES)
    weight_grad = lax.optimization_barrier(jnp.sum(w_terms, axis=0)) * grad_scale
    input_grad = lax.optimization_barrier(jnp.sum(v_terms, axis=0)) * grad_scale
    return (state_parts.reshape(NODES, KC), feature_parts.reshape(NODES, C), weight_grad, input_grad, sent_cot)
```

```python
import functools

import jax
import jax.numpy as jnp
from jax import lax
from jax.experimental import pallas as pl
from jax.experimental.pallas import tpu as pltpu
from jax.sharding import PartitionSpec as P

MESH = pl.DeviceIdType.MESH
F32 = jnp.float32
BF16 = jnp.bfloat16

STRIDE = {"x": 32, "z": 8, "y": 2}
ORDER = (("x", "z", "y"), ("z", "x", "y"), ("y", "x", "z"))
OFFSETS = (1, 2, 3, 4, -1, -2, -3, -4, 64)
SLOTS = 9
CAP = 64
NT = (((1,), (1,)), ((), ()))
TN = (((0,), (0,)), ((), ()))


def dot(a, b):
    return jnp.dot(a, b, preferred_element_type=F32)


def dot_nt(a, b):
    return lax.dot_general(a, b, NT, preferred_element_type=F32)


def dot_tn(a, b):
    return lax.dot_general(a, b, TN, preferred_element_type=F32)


def load_list(r):
    pairs = {}
    for i in range(4):
        rows = pl.ds(512 * i, 512)
        pairs["pa%d" % i] = (r["pre_act"].at[rows], r["pg"].at[rows])
        pairs["ct%d" % i] = (r["cotangent"].at[rows], r["ct"].at[rows])
    for name in ("send_idx", "tile_blocks", "coupling", "features", "w_input", "halo_states", "states", "halo_cot", "w_state"):
        pairs[name] = (r[name], r["v_" + name])
    return pairs


def start_loads(r):
    for at, (src, dst) in enumerate(load_list(r).values()):
        pltpu.make_async_copy(src, dst, r["in_sem"].at[at]).start()


def wait_load(r, name):
    pairs = load_list(r)
    at = list(pairs).index(name)
    pltpu.make_async_copy(*pairs[name], r["in_sem"].at[at]).wait()


def make_pre_grad(r):
    for i in range(4):
        wait_load(r, "pa%d" % i)
        wait_load(r, "ct%d" % i)

        @pl.loop(0, 4)
        def _(b):
            rows = pl.ds(pl.multiple_of(512 * i + 128 * b, 128), 128)
            third = (r["ct"][rows, :].astype(F32) * (1.0 / 3.0)).astype(BF16)
            for k in range(3):
                cols = slice(256 * k, 256 * k + 256)
                act = r["pg"][rows, cols]
                r["pg"][rows, cols] = jnp.where(act > 0, third, jnp.zeros_like(third))


def make_outgoing(r, out_ref):
    wait_load(r, "send_idx")

    @pl.loop(0, SLOTS)
    def _(j):
        rows = pl.ds(pl.multiple_of(64 * j, 64), 64)
        idx = r["v_send_idx"][rows, :]
        node = lax.broadcasted_iota(jnp.int32, (64, 2048), 1)
        r["oh"][rows, :] = jnp.where(node == idx, 1.0, 0.0).astype(BF16)

    for k in range(3):
        cols = slice(256 * k, 256 * k + 256)
        out_ref[:, cols] = dot(r["oh"][...], r["pg"][:, cols]).astype(BF16)


def make_feature_grad(r):
    wait_load(r, "w_input")

    @pl.loop(0, 4)
    def _(b):
        rows = pl.ds(pl.multiple_of(512 * b, 512), 512)
        total = dot_nt(r["pg"][rows, 0:256], r["v_w_input"][0])
        for k in (1, 2):
            total += dot_nt(r["pg"][rows, 256 * k : 256 * k + 256], r["v_w_input"][k])
        r["fo"][rows, :] = total.astype(BF16)


def make_v(r):
    wait_load(r, "features")
    r["gacc"][0] = jnp.zeros((3, 256, 256), F32)

    @pl.loop(0, 4)
    def _(b):
        rows = pl.ds(pl.multiple_of(512 * b, 512), 512)
        left = r["v_features"][rows, :].T
        for k in range(3):
            r["gacc"][0, k] += dot(left, r["pg"][rows, 256 * k : 256 * k + 256])


def mask_halo(r):
    wait_load(r, "halo_states")
    wait_load(r, "halo_cot")
    slot = lax.broadcasted_iota(jnp.int32, (CAP, 768), 0)
    for j in range(SLOTS):
        rows = slice(CAP * j, CAP * j + CAP)
        live = slot < r["recv_counts"][j]
        for name in ("v_halo_states", "v_halo_cot"):
            r[name][rows, :] = jnp.where(live, r[name][rows, :].astype(F32), 0.0).astype(BF16)


def make_d(r):
    wait_load(r, "coupling")
    r["dacc"][...] = jnp.zeros((576, 768), F32)

    @pl.loop(0, 4)
    def _(b):
        rows = pl.ds(pl.multiple_of(512 * b, 512), 512)
        left = r["v_coupling"][rows, :].T
        for k in range(3):
            cols = slice(256 * k, 256 * k + 256)
            r["dacc"][:, cols] += dot(left, r["pg"][rows, cols])


def flip_tiles(r):
    wait_load(r, "tile_blocks")

    @pl.loop(0, 16)
    def _(b):
        for i in range(4):
            r["v_tile_blocks"][b * 4 + i] = r["v_tile_blocks"][b * 4 + i].T


def make_q(r, k):
    cols = slice(256 * k, 256 * k + 256)
    meta = r["meta"]
    r["stage"][0] = jnp.zeros((128, 256), F32)

    @pl.loop(0, 64, unroll=8)
    def _(t):
        source = pl.ds(pl.multiple_of(meta[64 + t] * 128, 128), 128)
        product = dot(r["v_tile_blocks"][meta[t]], r["pg"][source, cols])
        keep = meta[128 + t] > 0
        r["stage"][t + 1] = product + jnp.where(keep, r["stage"][t], 0.0)

    @pl.loop(0, 16, unroll=4)
    def _(c):
        value = jnp.where(meta[208 + c] > 0, r["stage"][meta[192 + c]], 0.0)
        rows = pl.ds(pl.multiple_of(c * 128, 128), 128)
        r["qf"][rows, cols] = value
        r["qb"][rows, cols] = value.astype(BF16)


def make_w(r, k):
    cols = slice(256 * k, 256 * k + 256)
    r["gacc"][1, k] = dot_tn(r["v_halo_states"][:, cols], r["dacc"][:, cols].astype(BF16))

    @pl.loop(0, 2)
    def _(b):
        rows = pl.ds(pl.multiple_of(1024 * b, 1024), 1024)
        r["gacc"][1, k] += dot_tn(r["v_states"][rows, cols], r["qb"][rows, cols])


def make_state_grad(r):
    wait_load(r, "w_state")

    @pl.loop(0, 8)
    def _(b):
        rows = pl.ds(pl.multiple_of(256 * b, 256), 256)
        for k in range(3):
            cols = slice(256 * k, 256 * k + 256)
            pulled = dot(r["v_coupling"][rows, :], r["v_halo_cot"][:, cols]) + r["qf"][rows, cols]
            r["so"][rows, cols] = dot_nt(pulled.astype(BF16), r["v_w_state"][k]).astype(BF16)


def where_am_i():
    me = lax.axis_index("dom")
    at = {"x": me // 32, "z": (me // 8) % 4, "y": (me // 2) % 4}
    return me, me % 2, at


def peer(axis, j, flip):
    me, core, at = where_am_i()
    to = (at[axis] + j) % 4
    other = (core + flip) % 2
    return me + (to - at[axis]) * STRIDE[axis] + (other - core), to, other


def remote(src, dst, send, recv, device):
    return pltpu.make_async_remote_copy(src_ref=src, dst_ref=dst, send_sem=send, recv_sem=recv, device_id=(device,), device_id_type=MESH)


FIRST = [(j, f) for j in range(4) for f in range(2) if (j, f) != (0, 0)]


def greet():
    barrier = pltpu.get_barrier_semaphore()
    me, core, at = where_am_i()
    targets = [peer("x", 0, 1)[0]]
    for axis in ("x", "z", "y"):
        targets += [peer(axis, j, f)[0] for j in (1, 2, 3) for f in (0, 1)]
    targets += [(me + offset + 128) % 128 for offset in OFFSETS]
    for device in targets:
        pl.semaphore_signal(barrier, inc=1, device_id=(device,), device_id_type=MESH)
    return len(targets)


def await_greetings(count):
    pl.semaphore_wait(pltpu.get_barrier_semaphore(), count)


def halo_copy(r, j):
    me, _, _ = where_am_i()
    rows = pl.ds(CAP * j, CAP)
    return remote(r["outgoing"].at[rows], r["sent_cot"].at[rows], r["halo_send"].at[j], r["halo_recv"].at[j], (me + OFFSETS[j] + 128) % 128)


def rs8_copies(r, p, k):
    for slot, (j, f) in enumerate(FIRST):
        device, to, other = peer(ORDER[k][0], j, f)
        yield remote(r["gsend"].at[p, k, other * 4 + to], r["r1"].at[p, k, slot], r["s1_sem"].at[p, k, slot], r["r1_sem"].at[p, k, slot], device)


def rs4_copies(r, p, k):
    for j in (1, 2, 3):
        device, to, _ = peer(ORDER[k][1], j, 0)
        yield remote(r["s2"].at[p, k, to], r["r2"].at[p, k, j - 1], r["s2_sem"].at[p, k, j - 1], r["r2_sem"].at[p, k, j - 1], device)


def all4_copies(r, p, k):
    mine = where_am_i()[2][ORDER[k][2]]
    for j in (1, 2, 3):
        device, _, _ = peer(ORDER[k][2], j, 0)
        yield remote(r["r3"].at[p, k, mine], r["r3"].at[p, k, mine], r["s3_sem"].at[p, k, j - 1], r["r3_sem"].at[p, k, j - 1], device)


def ag4_copies(r, p, k):
    mine = where_am_i()[2][ORDER[k][1]]
    for j in (1, 2, 3):
        device, _, _ = peer(ORDER[k][1], j, 0)
        yield remote(r["ag4"].at[p, k, mine], r["ag4"].at[p, k, mine], r["s4_sem"].at[p, k, j - 1], r["r4_sem"].at[p, k, j - 1], device)


def ag8_copies(r, p, k):
    _, core, at = where_am_i()
    mine = core * 4 + at[ORDER[k][0]]
    for slot, (j, f) in enumerate(FIRST):
        device, _, _ = peer(ORDER[k][0], j, f)
        yield remote(r["ag4"].at[p, k], r["fin"].at[p, k, mine], r["s5_sem"].at[p, k, slot], r["r5_sem"].at[p, k, slot], device)


ALL = (rs8_copies, rs4_copies, all4_copies, ag4_copies, ag8_copies)


def start(copies):
    for copy in copies:
        copy.start()


def arrived(copies):
    for copy in copies:
        copy.wait_recv()


def reduce_start(r, p, k):
    for c in range(2):
        for a in range(4):
            block = r["gacc"][p, k, 64 * a : 64 * a + 64, 128 * c : 128 * c + 128]
            r["gsend"][p, k, c * 4 + a] = block.astype(BF16)
    start(rs8_copies(r, p, k))


def reduce_second(r, p, k):
    _, core, at = where_am_i()
    rows = pl.ds(pl.multiple_of(at[ORDER[k][0]] * 64, 64), 64)
    cols = pl.ds(pl.multiple_of(core * 128, 128), 128)
    total = r["gacc"][p, k, rows, cols]
    arrived(rs8_copies(r, p, k))
    for slot in range(7):
        total += r["r1"][p, k, slot].astype(F32)
    total = total.reshape(4, 16, 128)
    r["own2"][p, k] = total
    r["s2"][p, k] = total.astype(BF16)
    start(rs4_copies(r, p, k))


def reduce_third(r, p, k):
    at = where_am_i()[2]
    total = r["own2"][p, k, at[ORDER[k][1]]]
    arrived(rs4_copies(r, p, k))
    for slot in range(3):
        total += r["r2"][p, k, slot].astype(F32)
    r["r3"][p, k, at[ORDER[k][2]]] = total
    start(all4_copies(r, p, k))


def gather_start(r, p, k):
    at = where_am_i()[2]
    arrived(all4_copies(r, p, k))
    total = (r["r3"][p, k, 0] + r["r3"][p, k, 1]) + (r["r3"][p, k, 2] + r["r3"][p, k, 3])
    r["ag4"][p, k, at[ORDER[k][1]]] = total.astype(BF16)
    start(ag4_copies(r, p, k))


def gather_second(r, p, k):
    _, core, at = where_am_i()
    arrived(ag4_copies(r, p, k))
    start(ag8_copies(r, p, k))
    r["fin"][p, k, core * 4 + at[ORDER[k][0]]] = r["ag4"][p, k]


def gather_end(r, p, k, out_ref):
    arrived(ag8_copies(r, p, k))
    for c in range(2):
        for a in range(4):
            block = r["fin"][p, k, c * 4 + a].reshape(64, 128).astype(F32)
            out_ref[k, 64 * a : 64 * a + 64, 128 * c : 128 * c + 128] = block * (1.0 / 512.0)


def drain(r):
    for p in range(2):
        for k in range(3):
            for copies in ALL:
                for copy in copies(r, p, k):
                    copy.wait_send()


LINK_SCRATCH = dict(
    gsend=pltpu.VMEM((2, 3, 8, 64, 128), BF16),
    r1=pltpu.VMEM((2, 3, 7, 64, 128), BF16),
    own2=pltpu.VMEM((2, 3, 4, 16, 128), F32),
    s2=pltpu.VMEM((2, 3, 4, 16, 128), BF16),
    r2=pltpu.VMEM((2, 3, 3, 16, 128), BF16),
    r3=pltpu.VMEM((2, 3, 4, 16, 128), F32),
    ag4=pltpu.VMEM((2, 3, 4, 16, 128), BF16),
    fin=pltpu.VMEM((2, 3, 8, 4, 16, 128), BF16),
    s1_sem=pltpu.SemaphoreType.DMA((2, 3, 7)),
    r1_sem=pltpu.SemaphoreType.DMA((2, 3, 7)),
    s2_sem=pltpu.SemaphoreType.DMA((2, 3, 3)),
    r2_sem=pltpu.SemaphoreType.DMA((2, 3, 3)),
    s3_sem=pltpu.SemaphoreType.DMA((2, 3, 3)),
    r3_sem=pltpu.SemaphoreType.DMA((2, 3, 3)),
    s4_sem=pltpu.SemaphoreType.DMA((2, 3, 3)),
    r4_sem=pltpu.SemaphoreType.DMA((2, 3, 3)),
    s5_sem=pltpu.SemaphoreType.DMA((2, 3, 7)),
    r5_sem=pltpu.SemaphoreType.DMA((2, 3, 7)),
    halo_send=pltpu.SemaphoreType.DMA((9,)),
    halo_recv=pltpu.SemaphoreType.DMA((9,)),
)

LOCAL_SCRATCH = dict(
    pg=pltpu.VMEM((2048, 768), BF16),
    ct=pltpu.VMEM((2048, 256), BF16),
    v_send_idx=pltpu.VMEM((576, 1), jnp.int32),
    v_tile_blocks=pltpu.VMEM((64, 128, 128), BF16),
    v_coupling=pltpu.VMEM((2048, 576), BF16),
    v_features=pltpu.VMEM((2048, 256), BF16),
    v_w_input=pltpu.VMEM((3, 256, 256), BF16),
    v_halo_states=pltpu.VMEM((576, 768), BF16),
    v_states=pltpu.VMEM((2048, 768), BF16),
    v_halo_cot=pltpu.VMEM((576, 768), BF16),
    v_w_state=pltpu.VMEM((3, 256, 256), BF16),
    oh=pltpu.VMEM((576, 2048), BF16),
    dacc=pltpu.VMEM((576, 768), F32),
    stage=pltpu.VMEM((65, 128, 256), F32),
    qf=pltpu.VMEM((2048, 768), F32),
    qb=pltpu.VMEM((2048, 768), BF16),
    fo=pltpu.VMEM((2048, 256), BF16),
    so=pltpu.VMEM((2048, 768), BF16),
    in_sem=pltpu.SemaphoreType.DMA((17,)),
    out_sem=pltpu.SemaphoreType.DMA((2,)),
)

INPUTS = ("meta", "recv_counts", "states", "pre_act", "features", "cotangent", "halo_states", "halo_cot", "coupling", "tile_blocks", "send_idx", "w_state", "w_input")


def local_kernel(*refs):
    names = INPUTS + ("state_grad", "feature_grad", "gacc", "outgoing") + tuple(LOCAL_SCRATCH)
    r = dict(zip(names, refs, strict=True))
    start_loads(r)
    make_pre_grad(r)
    make_outgoing(r, r["outgoing"])
    make_feature_grad(r)
    out_f = pltpu.make_async_copy(r["fo"], r["feature_grad"], r["out_sem"].at[0])
    out_f.start()
    make_v(r)
    mask_halo(r)
    make_d(r)
    flip_tiles(r)
    wait_load(r, "states")
    for k in range(3):
        make_q(r, k)
        make_w(r, k)
    make_state_grad(r)
    out_s = pltpu.make_async_copy(r["so"], r["state_grad"], r["out_sem"].at[1])
    out_s.start()
    out_f.wait()
    out_s.wait()


def link_kernel(*refs):
    names = ("gacc", "outgoing", "weight_grad", "input_grad", "sent_cot") + tuple(LINK_SCRATCH)
    r = dict(zip(names, refs, strict=True))
    count = greet()
    await_greetings(count)
    order = [(p, k) for p in range(2) for k in range(3)]
    for p, k in order:
        reduce_start(r, p, k)
    for j in range(SLOTS):
        halo_copy(r, j).start()
    for step in (reduce_second, reduce_third, gather_start, gather_second):
        for p, k in order:
            step(r, p, k)
    for p, k in order:
        gather_end(r, p, k, r["weight_grad"] if p else r["input_grad"])
    drain(r)
    for j in range(SLOTS):
        halo_copy(r, j).wait()


def tile_order(tile_rows, tile_cols, tile_counts):
    slot = jnp.arange(64, dtype=jnp.int32)
    key = jnp.where(slot < tile_counts[0], tile_cols, 16)
    code = key * 64 + slot
    rank = jnp.sum((code[None, :] < code[:, None]).astype(jnp.int32), axis=1)
    place = (rank[None, :] == slot[:, None]).astype(jnp.int32)
    perm = jnp.sum(place * slot[None, :], axis=1)
    rows = jnp.sum(place * tile_rows[None, :], axis=1)
    keys = jnp.sum(place * key[None, :], axis=1)
    before = jnp.sum((rank[None, :] == slot[:, None] - 1).astype(jnp.int32) * (key[None, :] + 1), axis=1) - 1
    same = (keys == before).astype(jnp.int32)
    block = jnp.arange(16, dtype=jnp.int32)
    last = jnp.sum((key[None, :] <= block[:, None]).astype(jnp.int32), axis=1)
    some = jnp.sum((key[None, :] == block[:, None]).astype(jnp.int32), axis=1)
    return jnp.concatenate([perm, rows, same, last, some])


def shards(states, pre_act, features, cotangent, halo_states, halo_cot, coupling, tile_blocks, tile_rows, tile_cols, tile_counts, send_rows, send_counts, recv_counts, w_state, w_input):
    meta = tile_order(tile_rows, tile_cols, tile_counts)
    live = jnp.arange(CAP, dtype=jnp.int32)[None, :] < send_counts[:, None]
    send_idx = jnp.where(live, send_rows, -1).reshape(SLOTS * CAP, 1)
    any_spec = pl.BlockSpec(memory_space=pl.ANY)
    smem = pl.BlockSpec(memory_space=pltpu.SMEM)
    vmem = pl.BlockSpec(memory_space=pltpu.VMEM)
    state_grad, feature_grad, gacc, outgoing = pl.pallas_call(
        local_kernel,
        out_shape=(
            jax.ShapeDtypeStruct((2048, 768), BF16),
            jax.ShapeDtypeStruct((2048, 256), BF16),
            jax.ShapeDtypeStruct((2, 3, 256, 256), F32),
            jax.ShapeDtypeStruct((576, 768), BF16),
        ),
        in_specs=[smem, smem] + [any_spec] * (len(INPUTS) - 2),
        out_specs=(any_spec, any_spec, vmem, vmem),
        scratch_shapes=list(LOCAL_SCRATCH.values()),
        compiler_params=pltpu.CompilerParams(vmem_limit_bytes=60 * 2**20),
        name="local",
    )(meta, recv_counts, states, pre_act, features, cotangent, halo_states, halo_cot, coupling, tile_blocks, send_idx, w_state, w_input)
    weight_grad, input_grad, sent_cot = pl.pallas_call(
        link_kernel,
        out_shape=(
            jax.ShapeDtypeStruct((3, 256, 256), F32),
            jax.ShapeDtypeStruct((3, 256, 256), F32),
            jax.ShapeDtypeStruct((576, 768), BF16),
        ),
        in_specs=[vmem, vmem],
        out_specs=(vmem, vmem, any_spec),
        scratch_shapes=list(LINK_SCRATCH.values()),
        compiler_params=pltpu.CompilerParams(collective_id=0, has_side_effects=True, vmem_limit_bytes=40 * 2**20),
        name="links",
    )(gacc, outgoing)
    return (state_grad, feature_grad, weight_grad, input_grad, sent_cot)


def solution(mesh):
    rows = P("dom", None)
    one = P("dom")
    return jax.shard_map(
        shards,
        mesh=mesh,
        in_specs=(rows,) * 7 + (P("dom", None, None), one, one, one, rows, one, one, P(), P()),
        out_specs=(rows, rows, P(), P(), rows),
        check_vma=False,
    )
```

```python
from types import SimpleNamespace

import jax
import jax.numpy as jnp
from jax import lax
from jax.experimental import pallas as pl
from jax.experimental.pallas import tpu as pltpu
from jax.sharding import PartitionSpec as P

MESH = pl.DeviceIdType.MESH
F32 = jnp.float32
BF16 = jnp.bfloat16

OFFSETS = (1, 2, 3, 4, -1, -2, -3, -4, 64)
SLOTS = 9
CAP = 64
NT = (((1,), (1,)), ((), ()))
TN = (((0,), (0,)), ((), ()))


def dot(a, b):
    return jnp.dot(a, b, preferred_element_type=F32)


def dot_nt(a, b):
    return lax.dot_general(a, b, NT, preferred_element_type=F32)


def dot_tn(a, b):
    return lax.dot_general(a, b, TN, preferred_element_type=F32)


def order_tiles(r):
    r.load_tile_rows.wait()
    r.load_tile_cols.wait()
    count = r.tile_counts[0]
    sub = lax.broadcasted_iota(jnp.int32, (8, 128), 0)
    tile = lax.broadcasted_iota(jnp.int32, (64, 128), 0)
    lane = lax.broadcasted_iota(jnp.int32, (64, 128), 1)
    lane1 = lax.broadcasted_iota(jnp.int32, (1, 128), 1)
    zero = jnp.zeros((64, 128), jnp.int32)
    keys, rows = [], []
    for t in range(64):
        keys.append(jnp.where(t < count, r.s_tile_cols[t], 16))
        rows.append(r.s_tile_rows[t])

    def column(values):
        parts = []
        for b in range(8):
            part = jnp.zeros((8, 128), jnp.int32)
            for i in range(8):
                part = jnp.where(sub == i, values[8 * b + i], part)
            parts.append(part)
        return jnp.concatenate(parts, axis=0)

    key, row = column(keys), column(rows)
    place = zero
    for s in range(64):
        place += jnp.where((key == keys[s]) & (tile > s), 1, 0)
    base = zero
    upto = jnp.zeros((1, 128), jnp.int32)
    inside = jnp.zeros((1, 128), jnp.int32)
    for c in range(16):
        here = jnp.sum(jnp.where(key == c, 1, 0), axis=0, keepdims=True)
        pairs = (here + 1) >> 1
        base += jnp.where(key > c, pairs, 0)
        upto += jnp.where(lane1 >= c, pairs, 0)
        inside += jnp.where(lane1 == c, here, 0)
    at = jnp.where(key < 16, base + (place >> 1), 1000)
    first = (at == lane) & ((place & 1) == 0)
    second = (at == lane) & ((place & 1) == 1)

    def total(mask, value):
        return jnp.sum(jnp.where(mask, value, 0), axis=0, keepdims=True)

    meta = (total(first, tile - 64) + 64, total(second, tile - 64) + 64, total(first, row), total(second, row), total(first & (place > 0), 1), upto, inside)
    for i, value in enumerate(meta):
        r.v_meta[i : i + 1, :] = value
    r.v_meta[7:8, :] = jnp.zeros((1, 128), jnp.int32)
    pltpu.make_async_copy(r.v_meta, r.meta, r.meta_sem).start()


def make_pre_grad(r):
    for i in range(4):
        r.load_acts[i].wait()
        r.load_cots[i].wait()

        @pl.loop(0, 4)
        def _(b):
            rows = pl.ds(pl.multiple_of(512 * i + 128 * b, 128), 128)
            third = (r.ct[rows, :].astype(F32) * (1.0 / 3.0)).astype(BF16)
            for k in range(3):
                cols = slice(256 * k, 256 * k + 256)
                act = r.pg[rows, cols]
                r.pg[rows, cols] = jnp.where(act > 0, third, jnp.zeros_like(third))


def make_one_hot(r):
    r.load_send_rows.wait()
    index = r.v_send_rows[...].T
    slot = lax.broadcasted_iota(jnp.int32, (CAP, 1), 0)
    node = lax.broadcasted_iota(jnp.int32, (CAP, 2048), 1)
    for j in range(SLOTS):
        mine = jnp.where(slot < r.send_counts[j], index[:, j : j + 1], -1)
        r.oh[CAP * j : CAP * j + CAP, :] = jnp.where(node == mine, 1.0, 0.0).astype(BF16)


def make_outgoing(r, k):
    cols = slice(256 * k, 256 * k + 256)
    r.outgoing[:, cols] = dot(r.oh[...], r.pg[:, cols]).astype(BF16)


def make_feature_grad(r):
    @pl.loop(0, 2)
    def _(b):
        rows = pl.ds(pl.multiple_of(1024 * b, 1024), 1024)
        total = dot_nt(r.pg[rows, 0:256], r.w_input[0])
        for k in (1, 2):
            total += dot_nt(r.pg[rows, 256 * k : 256 * k + 256], r.w_input[k])
        r.feature_grad[rows, :] = total.astype(BF16)


def make_v(r):
    r.load_features.wait()
    for b in range(2):
        rows = pl.ds(1024 * b, 1024)
        left = r.v_features[rows, :].T
        for k in range(3):
            part = dot(left, r.pg[rows, 256 * k : 256 * k + 256])
            r.gacc[0, k] = part if b == 0 else r.gacc[0, k] + part


def mask_halo(r, ref):
    slot = lax.broadcasted_iota(jnp.int32, (CAP, 768), 0)
    for j in range(SLOTS):
        rows = slice(CAP * j, CAP * j + CAP)
        ref[rows, :] = jnp.where(slot < r.recv_counts[j], ref[rows, :].astype(F32), 0.0).astype(BF16)


def flip_tiles(r):
    r.v_tile_blocks[64] = jnp.zeros((128, 128), BF16)
    r.load_tile_blocks.wait()

    @pl.loop(0, 64, unroll=16)
    def _(t):
        r.v_tile_blocks[t] = r.v_tile_blocks[t].T


def make_q(r, k):
    cols = slice(256 * k, 256 * k + 256)
    meta, tiles = r.meta, r.v_tile_blocks

    @pl.loop(0, 40, unroll=20)
    def _(t):
        up = pl.ds(pl.multiple_of(meta[2, t] * 128, 128), 128)
        low = pl.ds(pl.multiple_of(meta[3, t] * 128, 128), 128)
        left = jnp.concatenate([tiles[meta[0, t]], tiles[meta[1, t]]], axis=1)
        right = jnp.concatenate([r.pg[up, cols], r.pg[low, cols]], axis=0)
        r.stage[t + 1] = dot(left, right) + jnp.where(meta[4, t] > 0, r.stage[t], 0.0)

    @pl.loop(0, 16, unroll=8)
    def _(c):
        value = jnp.where(meta[6, c] > 0, r.stage[meta[5, c]], 0.0)
        r.qb[pl.ds(pl.multiple_of(c * 128, 128), 128), cols] = value.astype(BF16)


def make_w(r, k):
    cols = slice(256 * k, 256 * k + 256)
    meet = dot(r.coupling[...], r.pg[:, cols]).astype(BF16)
    r.gacc[1, k] = dot_tn(r.v_halo_states[:, cols], meet)
    for b in range(2):
        rows = pl.ds(1024 * b, 1024)
        r.gacc[1, k] += dot_tn(r.states[rows, cols], r.qb[rows, cols])


def make_e(r):
    r.load_halo_cot.wait()
    mask_halo(r, r.v_halo_cot)
    for k in range(3):
        cols = slice(256 * k, 256 * k + 256)
        r.ee[:, cols] = dot_nt(r.v_halo_cot[:, cols], r.w_state[k]).astype(BF16)


def make_state_grad(r, half):
    @pl.loop(0, 2)
    def _(b):
        rows = pl.ds(pl.multiple_of(1024 * half + 512 * b, 512), 512)
        left = r.coupling[:, rows].T
        for k in range(3):
            cols = slice(256 * k, 256 * k + 256)
            total = dot(left, r.ee[:, cols]) + dot_nt(r.qb[rows, cols], r.w_state[k])
            r.state_grad[rows, cols] = total.astype(BF16)


class Place:
    def __init__(self):
        self.me = lax.axis_index("dom")
        self.x = lax.div(self.me, 32)
        self.z = lax.rem(lax.div(self.me, 8), 4)
        self.y = lax.rem(lax.div(self.me, 2), 4)
        self.core = lax.rem(self.me, 2)
        self.own = self.x * 4 + self.z
        self.xs = [lax.rem(self.x + j, 4) for j in range(4)]
        self.zs = [lax.rem(self.z + j, 4) for j in range(4)]
        self.sibling = self.me + 1 - 2 * self.core
        low = self.y * 2 + self.core
        self.plane = []
        for n in FAR_FIRST:
            to = self.xs[n // 4] * 4 + self.zs[n % 4]
            self.plane.append((n, to, to * 8 + low))
        base = self.me - self.y * 2
        self.line = [base + 2 * lax.rem(self.y + j, 4) for j in (1, 2, 3)]
        self.halo = [lax.rem(self.me + 128 + offset, 128) for offset in OFFSETS]


FAR_FIRST = (10, 6, 14, 9, 11, 5, 7, 13, 15, 2, 8, 1, 3, 4, 12)


def remote(src, dst, send, recv, device):
    return pltpu.make_async_remote_copy(src_ref=src, dst_ref=dst, send_sem=send, recv_sem=recv, device_id=(device,), device_id_type=MESH)


def greet(at):
    barrier = pltpu.get_barrier_semaphore()
    for device in [at.sibling] + [device for _, _, device in at.plane] + at.line + at.halo:
        pl.semaphore_signal(barrier, inc=1, device_id=(device,), device_id_type=MESH)


def await_greetings():
    pl.semaphore_wait(pltpu.get_barrier_semaphore(), 1 + 15 + 3 + SLOTS)


def halo_copy(r, at, j):
    rows = pl.ds(CAP * j, CAP)
    return remote(r.outgoing.at[rows], r.sent_cot.at[rows], r.halo_send.at[j], r.halo_recv.at[j], at.halo[j])


def core_copy(at, g):
    return remote(g.half, g.core, g.a_send, g.a_recv, at.sibling)


def scatter_all(at, g):
    return remote(g.r1, g.r1, g.b_send, g.b_recv, at.sibling)


def line_copy(at, g, j):
    mine = g.r2.at[at.y]
    return remote(mine, mine, g.c_send.at[j], g.c_recv.at[j], at.line[j])


def gather_all(at, g):
    every = g.fin.at[0, pl.ds(0, 15)]
    return remote(every, every, g.d_send, g.d_recv, at.sibling)


def sibling_copy(at, g):
    mine = g.fin.at[at.core]
    return remote(mine, mine, g.e_send, g.e_recv, at.sibling)


def reduce_core(r, at, g):
    theirs = pl.ds(pl.multiple_of((1 - at.core) * 128, 128), 128)
    for i in range(g.count):
        g.half[i] = r.gacc[g.p, g.k + i, :, theirs].astype(BF16)
    core_copy(at, g).start()


def reduce_plane(r, at, g):
    ours = pl.ds(pl.multiple_of(at.core * 128, 128), 128)
    core_copy(at, g).wait_recv()
    for i in range(g.count):
        total = r.gacc[g.p, g.k + i, :, ours] + g.core[i].astype(F32)
        g.sum[i] = total
        g.send[:, i] = total.reshape(16, 16, 128).astype(BF16)
    for n, to, device in at.plane:
        remote(g.send.at[to], g.r1.at[n - 1], g.b_send, g.b_recv, device).start()


def reduce_line(r, at, g):
    rows = pl.ds(pl.multiple_of(at.own * 16, 16), 16)
    total = g.sum[:, rows, :]
    scatter_all(at, g).wait_recv()
    for n in range(15):
        total += g.r1[n].astype(F32)
    g.r2[at.y] = total
    for j in range(3):
        line_copy(at, g, j).start()


def gather_plane(r, at, g):
    for j in range(3):
        line_copy(at, g, j).wait_recv()
    total = (g.r2[0] + g.r2[1]) + (g.r2[2] + g.r2[3])
    g.fin[at.core, at.own] = total.astype(BF16)
    mine = g.fin.at[at.core, at.own]
    for _, _, device in at.plane:
        remote(mine, mine, g.d_send, g.d_recv, device).start()


def gather_core(r, at, g):
    gather_all(at, g).wait_recv()
    sibling_copy(at, g).start()


def gather_end(r, at, g):
    out = r.weight_grad if g.p else r.input_grad
    sibling_copy(at, g).wait_recv()
    for i in range(g.count):
        for c in range(2):
            block = g.fin[c, :, i].astype(F32).reshape(256, 128)
            out[g.k + i, :, 128 * c : 128 * c + 128] = block * (1.0 / 512.0)


def drain(r, at):
    for g in r.groups:
        core_copy(at, g).wait_send()
        scatter_all(at, g).wait_send()
        for j in range(3):
            line_copy(at, g, j).wait_send()
        gather_all(at, g).wait_send()
        sibling_copy(at, g).wait_send()
    for j in range(SLOTS):
        halo_copy(r, at, j).wait()


GROUPS = ((0, 0, 3), (1, 0, 1), (1, 1, 1), (1, 2, 1))
DMA = pltpu.SemaphoreType.DMA


def group_scratch(count):
    one = DMA(())
    return dict(
        half=pltpu.VMEM((count, 256, 128), BF16),
        core=pltpu.VMEM((count, 256, 128), BF16),
        sum=pltpu.VMEM((count, 256, 128), F32),
        send=pltpu.VMEM((16, count, 16, 128), BF16),
        r1=pltpu.VMEM((15, count, 16, 128), BF16),
        r2=pltpu.VMEM((4, count, 16, 128), F32),
        fin=pltpu.VMEM((2, 16, count, 16, 128), BF16),
        a_send=one, a_recv=one, b_send=one, b_recv=one, c_send=DMA((3,)), c_recv=DMA((3,)),
        d_send=one, d_recv=one, e_send=one, e_recv=one,
    )


TILES_SCRATCH = dict(
    ct=pltpu.VMEM((2048, 256), BF16),
    v_tile_blocks=pltpu.VMEM((65, 128, 128), BF16),
    stage=pltpu.VMEM((41, 128, 256), F32),
    meta=pltpu.SMEM((8, 128), jnp.int32),
    v_meta=pltpu.VMEM((8, 128), jnp.int32),
    s_tile_rows=pltpu.SMEM((64,), jnp.int32),
    s_tile_cols=pltpu.SMEM((64,), jnp.int32),
    in_sem=DMA((11,)),
    meta_sem=DMA(()),
)


def tiles_kernel(tile_counts, tile_rows, tile_cols, pre_act, cotangent, tile_blocks, pg, qb, *scratch):
    r = SimpleNamespace(**dict(zip(TILES_SCRATCH, scratch, strict=True)), tile_counts=tile_counts, pg=pg, qb=qb)

    def load(i, src, dst):
        copy = pltpu.make_async_copy(src, dst, r.in_sem.at[i])
        copy.start()
        return copy

    r.load_tile_rows = load(0, tile_rows, r.s_tile_rows)
    r.load_tile_cols = load(1, tile_cols, r.s_tile_cols)
    parts = [pl.ds(512 * i, 512) for i in range(4)]
    r.load_cots, r.load_acts = [], []
    for i, rows in enumerate(parts):
        r.load_cots.append(load(2 + i, cotangent.at[rows], r.ct.at[rows]))
        r.load_acts.append(load(6 + i, pre_act.at[rows], pg.at[rows]))
    r.load_tile_blocks = load(10, tile_blocks, r.v_tile_blocks.at[pl.ds(0, 64)])
    order_tiles(r)
    r.stage[0] = jnp.zeros((128, 256), F32)
    make_pre_grad(r)
    flip_tiles(r)
    pltpu.make_async_copy(r.v_meta, r.meta, r.meta_sem).wait()
    for k in range(3):
        make_q(r, k)


REST_SCRATCH = dict(
    v_send_rows=pltpu.VMEM((9, 64), jnp.int32),
    v_features=pltpu.VMEM((2048, 256), BF16),
    v_halo_states=pltpu.VMEM((576, 768), BF16),
    v_halo_cot=pltpu.VMEM((576, 768), BF16),
    oh=pltpu.VMEM((576, 2048), BF16),
    ee=pltpu.VMEM((576, 768), BF16),
    outgoing=pltpu.VMEM((576, 768), BF16),
    gacc=pltpu.VMEM((2, 3, 256, 256), F32),
    in_sem=DMA((4,)),
    halo_send=DMA((9,)),
    halo_recv=DMA((9,)),
)


def rest_refs(send_counts, recv_counts, pg, qb, states, features, halo_states, halo_cot, coupling, send_rows, w_state, w_input, state_grad, feature_grad, weight_grad, input_grad, sent_cot, *scratch):
    scratch = list(scratch)
    own = dict(zip(REST_SCRATCH, scratch))
    del scratch[: len(own)]
    r = SimpleNamespace(**own, send_counts=send_counts, recv_counts=recv_counts, pg=pg, qb=qb, states=states, coupling=coupling, w_state=w_state, w_input=w_input)
    r.state_grad, r.feature_grad, r.weight_grad, r.input_grad, r.sent_cot = state_grad, feature_grad, weight_grad, input_grad, sent_cot
    r.groups = []
    for p, k, count in GROUPS:
        kinds = group_scratch(count)
        r.groups.append(SimpleNamespace(**dict(zip(kinds, scratch)), p=p, k=k, count=count))
        del scratch[: len(kinds)]

    def load(i, src, dst):
        copy = pltpu.make_async_copy(src, dst, r.in_sem.at[i])
        copy.start()
        return copy

    r.load_halo_states = load(0, halo_states, r.v_halo_states)
    r.load_features = load(1, features, r.v_features)
    r.load_send_rows = load(2, send_rows, r.v_send_rows)
    r.load_halo_cot = load(3, halo_cot, r.v_halo_cot)
    return r


def rest_kernel(*refs):
    r = rest_refs(*refs)
    v, w0, w1, w2 = r.groups
    at = Place()
    greet(at)

    def halo(*slots):
        for j in slots:
            halo_copy(r, at, j).start()

    r.load_halo_states.wait()
    mask_halo(r, r.v_halo_states)
    make_w(r, 0)
    await_greetings()
    reduce_core(r, at, w0)
    make_w(r, 1)
    reduce_core(r, at, w1)
    reduce_plane(r, at, w0)
    make_w(r, 2)
    reduce_core(r, at, w2)
    reduce_plane(r, at, w1)
    make_v(r)
    reduce_core(r, at, v)
    reduce_plane(r, at, w2)
    make_one_hot(r)
    make_outgoing(r, 0)
    reduce_line(r, at, w0)
    reduce_plane(r, at, v)
    make_outgoing(r, 1)
    make_outgoing(r, 2)
    halo(2, 6)
    reduce_line(r, at, w1)
    make_e(r)
    reduce_line(r, at, w2)
    gather_plane(r, at, w0)
    halo(3, 7)
    make_feature_grad(r)
    gather_plane(r, at, w1)
    reduce_line(r, at, v)
    make_state_grad(r, 0)
    gather_plane(r, at, w2)
    halo(1, 5)
    gather_core(r, at, w0)
    make_state_grad(r, 1)
    gather_plane(r, at, v)
    halo(0, 4, 8)
    gather_end(r, at, w0)
    gather_core(r, at, w1)
    gather_core(r, at, w2)
    gather_end(r, at, w1)
    gather_end(r, at, w2)
    gather_core(r, at, v)
    gather_end(r, at, v)
    drain(r, at)


def move_kernel(*refs):
    sem = refs[-1]
    copies = [pltpu.make_async_copy(refs[i], refs[5 + i], sem.at[i]) for i in range(5)]
    for copy in copies:
        copy.start()
    for copy in copies:
        copy.wait()


def shards(states, pre_act, features, cotangent, halo_states, halo_cot, coupling, tile_blocks, tile_rows, tile_cols, tile_counts, send_rows, send_counts, recv_counts, w_state, w_input):
    far = pl.BlockSpec(memory_space=pl.ANY)
    smem = pl.BlockSpec(memory_space=pltpu.SMEM)
    vmem = pl.BlockSpec(memory_space=pltpu.VMEM)
    wide = jax.ShapeDtypeStruct((2048, 768), BF16)
    results = (
        wide,
        jax.ShapeDtypeStruct((2048, 256), BF16),
        jax.ShapeDtypeStruct((3, 256, 256), F32),
        jax.ShapeDtypeStruct((3, 256, 256), F32),
        jax.ShapeDtypeStruct((576, 768), BF16),
    )
    hbm = pl.BlockSpec(memory_space=pltpu.HBM)

    def stay(value):
        return pltpu.with_memory_space_constraint(value, pltpu.HBM)

    pg, qb = pl.pallas_call(
        tiles_kernel,
        out_shape=(wide, wide),
        in_specs=[smem] + [hbm] * 5,
        out_specs=(vmem, vmem),
        scratch_shapes=list(TILES_SCRATCH.values()),
        compiler_params=pltpu.CompilerParams(vmem_limit_bytes=TILES_LIMIT * 2**20),
        name="tiles",
    )(tile_counts, *[stay(v) for v in (tile_rows, tile_cols, pre_act, cotangent, tile_blocks)])
    found = pl.pallas_call(
        rest_kernel,
        out_shape=results,
        in_specs=[smem] * 2 + [vmem] * 3 + [hbm] * 3 + [vmem, hbm, vmem, vmem],
        out_specs=(vmem,) * 5,
        scratch_shapes=list(REST_SCRATCH.values()) + [kind for group in GROUPS for kind in group_scratch(group[2]).values()],
        compiler_params=pltpu.CompilerParams(collective_id=0, has_side_effects=True, vmem_limit_bytes=REST_LIMIT * 2**20),
        name="rest",
    )(send_counts, recv_counts, pg, qb, states, stay(features), stay(halo_states), stay(halo_cot), coupling.T, stay(send_rows), w_state, w_input)
    return pl.pallas_call(
        move_kernel,
        out_shape=results,
        in_specs=[vmem] * 5,
        out_specs=(far,) * 5,
        scratch_shapes=[pltpu.SemaphoreType.DMA((5,))],
        compiler_params=pltpu.CompilerParams(vmem_limit_bytes=2**20),
        name="move",
    )(*found)


TILES_LIMIT = 20
REST_LIMIT = 24


def solution(mesh):
    rows = P("dom", None)
    one = P("dom")
    return jax.shard_map(
        shards,
        mesh=mesh,
        in_specs=(rows,) * 7 + (P("dom", None, None), one, one, one, rows, one, one, P(), P()),
        out_specs=(rows, rows, P(), P(), rows),
        check_vma=False,
    )
```

```python
from types import SimpleNamespace

import jax
import jax.numpy as jnp
from jax import lax
from jax.experimental import pallas as pl
from jax.experimental.pallas import tpu as pltpu
from jax.sharding import PartitionSpec as P

MESH = pl.DeviceIdType.MESH
F32 = jnp.float32
BF16 = jnp.bfloat16

OFFSETS = (1, 2, 3, 4, -1, -2, -3, -4, 64)
SLOTS = 9
CAP = 64
NT = (((1,), (1,)), ((), ()))
TN = (((0,), (0,)), ((), ()))


def dot(a, b):
    return jnp.dot(a, b, preferred_element_type=F32)


def dot_nt(a, b):
    return lax.dot_general(a, b, NT, preferred_element_type=F32)


def dot_tn(a, b):
    return lax.dot_general(a, b, TN, preferred_element_type=F32)


def order_tiles(r):
    r.load_tile_rows.wait()
    r.load_tile_cols.wait()
    count = r.tile_counts[0]
    sub = lax.broadcasted_iota(jnp.int32, (8, 128), 0)
    tile = lax.broadcasted_iota(jnp.int32, (64, 128), 0)
    lane = lax.broadcasted_iota(jnp.int32, (64, 128), 1)
    lane1 = lax.broadcasted_iota(jnp.int32, (1, 128), 1)
    zero = jnp.zeros((64, 128), jnp.int32)
    keys, rows = [], []
    for t in range(64):
        keys.append(jnp.where(t < count, r.s_tile_cols[t], 16))
        rows.append(r.s_tile_rows[t])

    def column(values):
        parts = []
        for b in range(8):
            part = jnp.zeros((8, 128), jnp.int32)
            for i in range(8):
                part = jnp.where(sub == i, values[8 * b + i], part)
            parts.append(part)
        return jnp.concatenate(parts, axis=0)

    key, row = column(keys), column(rows)
    place = zero
    for s in range(64):
        place += jnp.where((key == keys[s]) & (tile > s), 1, 0)
    base = zero
    upto = jnp.zeros((1, 128), jnp.int32)
    inside = jnp.zeros((1, 128), jnp.int32)
    for c in range(16):
        here = jnp.sum(jnp.where(key == c, 1, 0), axis=0, keepdims=True)
        pairs = (here + 1) >> 1
        base += jnp.where(key > c, pairs, 0)
        upto += jnp.where(lane1 >= c, pairs, 0)
        inside += jnp.where(lane1 == c, here, 0)
    at = jnp.where(key < 16, base + (place >> 1), 1000)
    first = (at == lane) & ((place & 1) == 0)
    second = (at == lane) & ((place & 1) == 1)

    def total(mask, value):
        return jnp.sum(jnp.where(mask, value, 0), axis=0, keepdims=True)

    meta = (total(first, tile - 64) + 64, total(second, tile - 64) + 64, total(first, row), total(second, row), total(first & (place > 0), 1), upto, jnp.minimum(inside, 1))
    for i, value in enumerate(meta):
        r.meta[i : i + 1, :] = value
    r.meta[7:8, :] = jnp.zeros((1, 128), jnp.int32)


def make_pre_grad(r):
    for i in range(4):
        r.load_acts[i].wait()
        r.load_cots[i].wait()

        @pl.loop(0, 4)
        def _(b):
            rows = pl.ds(pl.multiple_of(512 * i + 128 * b, 128), 128)
            third = (r.ct[rows, :].astype(F32) * (1.0 / 3.0)).astype(BF16)
            for k in range(3):
                cols = slice(256 * k, 256 * k + 256)
                act = r.pg[rows, cols]
                r.pg[rows, cols] = jnp.where(act > 0, third, jnp.zeros_like(third))


def make_one_hot(r):
    r.load_send_rows.wait()
    index = r.v_send_rows[...].T
    slot = lax.broadcasted_iota(jnp.int32, (CAP, 1), 0)
    node = lax.broadcasted_iota(jnp.int32, (CAP, 2048), 1)
    for j in range(SLOTS):
        mine = jnp.where(slot < r.send_counts[j], index[:, j : j + 1], -1)
        r.oh[CAP * j : CAP * j + CAP, :] = jnp.where(node == mine, 1.0, 0.0).astype(BF16)


def make_outgoing(r, k):
    cols = slice(256 * k, 256 * k + 256)
    r.outgoing[:, cols] = dot(r.oh[...], r.pg[:, cols]).astype(BF16)


def make_feature_grad(r):
    @pl.loop(0, 2)
    def _(b):
        rows = pl.ds(pl.multiple_of(1024 * b, 1024), 1024)
        total = dot_nt(r.pg[rows, 0:256], r.w_input[0])
        for k in (1, 2):
            total += dot_nt(r.pg[rows, 256 * k : 256 * k + 256], r.w_input[k])
        r.feature_grad[rows, :] = total.astype(BF16)


def make_v(r):
    r.load_features.wait()
    for b in range(2):
        rows = pl.ds(1024 * b, 1024)
        left = r.v_features[rows, :].T
        for k in range(3):
            part = dot(left, r.pg[rows, 256 * k : 256 * k + 256])
            r.gacc[0, k] = part if b == 0 else r.gacc[0, k] + part


def mask_halo(r, ref):
    slot = lax.broadcasted_iota(jnp.int32, (CAP, 768), 0)
    for j in range(SLOTS):
        rows = slice(CAP * j, CAP * j + CAP)
        ref[rows, :] = jnp.where(slot < r.recv_counts[j], ref[rows, :].astype(F32), 0.0).astype(BF16)


def flip_tiles(r):
    r.tiles[64] = jnp.zeros((128, 128), BF16)
    r.load_tile_blocks.wait()

    @pl.loop(0, 64, unroll=16)
    def _(t):
        r.tiles[t] = r.tiles[t].T


def make_q(r, k):
    cols = slice(256 * k, 256 * k + 256)
    meta, tiles = r.meta, r.tiles

    @pl.loop(0, 40, unroll=20)
    def _(t):
        left = jnp.concatenate([tiles[meta[0, t]], tiles[meta[1, t]]], axis=1)
        right = jnp.concatenate([r.blocked[meta[2, t], :, cols], r.blocked[meta[3, t], :, cols]], axis=0)
        r.stage[t + 1] = dot(left, right) + r.stage[t] * meta[4, t].astype(F32)

    @pl.loop(0, 16, unroll=8)
    def _(c):
        value = r.stage[meta[5, c]] * meta[6, c].astype(F32)
        r.qb[pl.ds(pl.multiple_of(c * 128, 128), 128), cols] = value.astype(BF16)


def make_w(r, k):
    cols = slice(256 * k, 256 * k + 256)
    meet = dot(r.coupling[...], r.pg[:, cols]).astype(BF16)
    r.gacc[1, k] = dot_tn(r.v_halo_states[:, cols], meet)
    for b in range(2):
        rows = pl.ds(1024 * b, 1024)
        r.gacc[1, k] += dot_tn(r.states[rows, cols], r.qb[rows, cols])


def make_e(r):
    r.load_halo_cot.wait()
    mask_halo(r, r.v_halo_cot)
    for k in range(3):
        cols = slice(256 * k, 256 * k + 256)
        r.ee[:, cols] = dot_nt(r.v_halo_cot[:, cols], r.w_state[k]).astype(BF16)


def make_state_grad(r, half):
    @pl.loop(0, 2)
    def _(b):
        rows = pl.ds(pl.multiple_of(1024 * half + 512 * b, 512), 512)
        left = r.coupling[:, rows].T
        for k in range(3):
            cols = slice(256 * k, 256 * k + 256)
            total = dot(left, r.ee[:, cols]) + dot_nt(r.qb[rows, cols], r.w_state[k])
            r.state_grad[rows, cols] = total.astype(BF16)


class Place:
    def __init__(self):
        self.me = lax.axis_index("dom")
        self.x = lax.div(self.me, 32)
        self.z = lax.rem(lax.div(self.me, 8), 4)
        self.y = lax.rem(lax.div(self.me, 2), 4)
        self.core = lax.rem(self.me, 2)
        self.own = self.x * 4 + self.z
        self.xs = [lax.rem(self.x + j, 4) for j in range(4)]
        self.zs = [lax.rem(self.z + j, 4) for j in range(4)]
        self.sibling = self.me + 1 - 2 * self.core
        low = self.y * 2 + self.core
        self.plane = []
        for n in FAR_FIRST:
            to = self.xs[n // 4] * 4 + self.zs[n % 4]
            self.plane.append((n, to, to * 8 + low))
        base = self.me - self.y * 2
        self.line = [base + 2 * lax.rem(self.y + j, 4) for j in (1, 2, 3)]
        self.halo = [lax.rem(self.me + 128 + offset, 128) for offset in OFFSETS]


FAR_FIRST = (10, 6, 14, 9, 11, 5, 7, 13, 15, 2, 8, 1, 3, 4, 12)


def remote(src, dst, send, recv, device):
    return pltpu.make_async_remote_copy(src_ref=src, dst_ref=dst, send_sem=send, recv_sem=recv, device_id=(device,), device_id_type=MESH)


def greet(at):
    barrier = pltpu.get_barrier_semaphore()
    for device in [at.sibling] + [device for _, _, device in at.plane] + at.line + at.halo:
        pl.semaphore_signal(barrier, inc=1, device_id=(device,), device_id_type=MESH)


def await_greetings():
    pl.semaphore_wait(pltpu.get_barrier_semaphore(), 1 + 15 + 3 + SLOTS)


def halo_copy(r, at, j):
    rows = pl.ds(CAP * j, CAP)
    return remote(r.outgoing.at[rows], r.sent_cot.at[rows], r.halo_send.at[j], r.halo_recv.at[j], at.halo[j])


def core_copy(at, g):
    return remote(g.half, g.core, g.a_send, g.a_recv, at.sibling)


def scatter_all(at, g):
    return remote(g.r1, g.r1, g.b_send, g.b_recv, at.sibling)


def line_copy(at, g, j):
    mine = g.r2.at[at.y]
    return remote(mine, mine, g.c_send.at[j], g.c_recv.at[j], at.line[j])


def gather_all(at, g):
    every = g.fin.at[0, pl.ds(0, 15)]
    return remote(every, every, g.d_send, g.d_recv, at.sibling)


def sibling_copy(at, g):
    mine = g.fin.at[at.core]
    return remote(mine, mine, g.e_send, g.e_recv, at.sibling)


def reduce_core(r, at, g):
    theirs = pl.ds(pl.multiple_of((1 - at.core) * 128, 128), 128)
    for i in range(g.count):
        g.half[i] = r.gacc[g.p, g.k + i, :, theirs].astype(BF16)
    core_copy(at, g).start()


def reduce_plane(r, at, g):
    ours = pl.ds(pl.multiple_of(at.core * 128, 128), 128)
    core_copy(at, g).wait_recv()
    for i in range(g.count):
        total = r.gacc[g.p, g.k + i, :, ours] + g.core[i].astype(F32)
        g.sum[i] = total
        g.send[:, i] = total.reshape(16, 16, 128).astype(BF16)
    for n, to, device in at.plane:
        remote(g.send.at[to], g.r1.at[n - 1], g.b_send, g.b_recv, device).start()


def reduce_line(r, at, g):
    rows = pl.ds(pl.multiple_of(at.own * 16, 16), 16)
    total = g.sum[:, rows, :]
    scatter_all(at, g).wait_recv()
    for n in range(15):
        total += g.r1[n].astype(F32)
    g.r2[at.y] = total
    for j in range(3):
        line_copy(at, g, j).start()


def gather_plane(r, at, g):
    for j in range(3):
        line_copy(at, g, j).wait_recv()
    total = (g.r2[0] + g.r2[1]) + (g.r2[2] + g.r2[3])
    g.fin[at.core, at.own] = total.astype(BF16)
    mine = g.fin.at[at.core, at.own]
    for _, _, device in at.plane:
        remote(mine, mine, g.d_send, g.d_recv, device).start()


def gather_core(r, at, g):
    gather_all(at, g).wait_recv()
    sibling_copy(at, g).start()


def gather_end(r, at, g):
    out = r.weight_grad if g.p else r.input_grad
    sibling_copy(at, g).wait_recv()
    for i in range(g.count):
        for c in range(2):
            block = g.fin[c, :, i].astype(F32).reshape(256, 128)
            out[g.k + i, :, 128 * c : 128 * c + 128] = block * (1.0 / 512.0)


def drain(r, at):
    for g in r.groups:
        core_copy(at, g).wait_send()
        scatter_all(at, g).wait_send()
        for j in range(3):
            line_copy(at, g, j).wait_send()
        gather_all(at, g).wait_send()
        sibling_copy(at, g).wait_send()
    for j in range(SLOTS):
        halo_copy(r, at, j).wait()


GROUPS = ((0, 0, 3), (1, 0, 1), (1, 1, 1), (1, 2, 1))
DMA = pltpu.SemaphoreType.DMA


def group_scratch(count):
    one = DMA(())
    return dict(
        half=pltpu.VMEM((count, 256, 128), BF16),
        core=pltpu.VMEM((count, 256, 128), BF16),
        sum=pltpu.VMEM((count, 256, 128), F32),
        send=pltpu.VMEM((16, count, 16, 128), BF16),
        r1=pltpu.VMEM((15, count, 16, 128), BF16),
        r2=pltpu.VMEM((4, count, 16, 128), F32),
        fin=pltpu.VMEM((2, 16, count, 16, 128), BF16),
        a_send=one, a_recv=one, b_send=one, b_recv=one, c_send=DMA((3,)), c_recv=DMA((3,)),
        d_send=one, d_recv=one, e_send=one, e_recv=one,
    )


FIRST_SCRATCH = dict(
    ct=pltpu.VMEM((2048, 256), BF16),
    s_tile_rows=pltpu.SMEM((64,), jnp.int32),
    s_tile_cols=pltpu.SMEM((64,), jnp.int32),
    in_sem=DMA((11,)),
)


def first_kernel(tile_counts, tile_rows, tile_cols, pre_act, cotangent, tile_blocks, pg, tiles, meta, *scratch):
    r = SimpleNamespace(**dict(zip(FIRST_SCRATCH, scratch, strict=True)), tile_counts=tile_counts, pg=pg, tiles=tiles, meta=meta)

    def load(i, src, dst):
        copy = pltpu.make_async_copy(src, dst, r.in_sem.at[i])
        copy.start()
        return copy

    r.load_tile_rows = load(0, tile_rows, r.s_tile_rows)
    r.load_tile_cols = load(1, tile_cols, r.s_tile_cols)
    parts = [pl.ds(512 * i, 512) for i in range(4)]
    r.load_cots, r.load_acts = [], []
    for i, rows in enumerate(parts):
        r.load_cots.append(load(2 + i, cotangent.at[rows], r.ct.at[rows]))
        r.load_acts.append(load(6 + i, pre_act.at[rows], pg.at[rows]))
    r.load_tile_blocks = load(10, tile_blocks, tiles.at[pl.ds(0, 64)])
    order_tiles(r)
    make_pre_grad(r)
    flip_tiles(r)


REST_SCRATCH = dict(
    stage=pltpu.VMEM((41, 128, 256), F32),
    qb=pltpu.VMEM((2048, 768), BF16),
    v_send_rows=pltpu.VMEM((9, 64), jnp.int32),
    v_features=pltpu.VMEM((2048, 256), BF16),
    v_halo_states=pltpu.VMEM((576, 768), BF16),
    v_halo_cot=pltpu.VMEM((576, 768), BF16),
    oh=pltpu.VMEM((576, 2048), BF16),
    ee=pltpu.VMEM((576, 768), BF16),
    outgoing=pltpu.VMEM((576, 768), BF16),
    gacc=pltpu.VMEM((2, 3, 256, 256), F32),
    in_sem=DMA((4,)),
    halo_send=DMA((9,)),
    halo_recv=DMA((9,)),
)


def rest_refs(send_counts, recv_counts, meta, pg, blocked, tiles, states, features, halo_states, halo_cot, coupling, send_rows, w_state, w_input, state_grad, feature_grad, weight_grad, input_grad, sent_cot, *scratch):
    scratch = list(scratch)
    own = dict(zip(REST_SCRATCH, scratch))
    del scratch[: len(own)]
    r = SimpleNamespace(**own, send_counts=send_counts, recv_counts=recv_counts, meta=meta, pg=pg, blocked=blocked, tiles=tiles, states=states, coupling=coupling, w_state=w_state, w_input=w_input)
    r.state_grad, r.feature_grad, r.weight_grad, r.input_grad, r.sent_cot = state_grad, feature_grad, weight_grad, input_grad, sent_cot
    r.groups = []
    for p, k, count in GROUPS:
        kinds = group_scratch(count)
        r.groups.append(SimpleNamespace(**dict(zip(kinds, scratch)), p=p, k=k, count=count))
        del scratch[: len(kinds)]

    def load(i, src, dst):
        copy = pltpu.make_async_copy(src, dst, r.in_sem.at[i])
        copy.start()
        return copy

    r.load_halo_states = load(0, halo_states, r.v_halo_states)
    r.load_features = load(1, features, r.v_features)
    r.load_send_rows = load(2, send_rows, r.v_send_rows)
    r.load_halo_cot = load(3, halo_cot, r.v_halo_cot)
    return r


def rest_kernel(*refs):
    r = rest_refs(*refs)
    v, w0, w1, w2 = r.groups
    at = Place()
    greet(at)

    def halo(*slots):
        for j in slots:
            halo_copy(r, at, j).start()

    r.stage[0] = jnp.zeros((128, 256), F32)
    make_q(r, 0)
    r.load_halo_states.wait()
    mask_halo(r, r.v_halo_states)
    make_w(r, 0)
    await_greetings()
    reduce_core(r, at, w0)
    make_q(r, 1)
    make_w(r, 1)
    reduce_core(r, at, w1)
    reduce_plane(r, at, w0)
    make_q(r, 2)
    make_w(r, 2)
    reduce_core(r, at, w2)
    reduce_plane(r, at, w1)
    make_v(r)
    reduce_core(r, at, v)
    reduce_plane(r, at, w2)
    make_one_hot(r)
    make_outgoing(r, 0)
    reduce_line(r, at, w0)
    reduce_plane(r, at, v)
    make_outgoing(r, 1)
    make_outgoing(r, 2)
    reduce_line(r, at, w1)
    halo(3, 7)
    make_e(r)
    make_feature_grad(r)
    reduce_line(r, at, w2)
    gather_plane(r, at, w0)
    halo(2, 6)
    make_state_grad(r, 0)
    reduce_line(r, at, v)
    gather_plane(r, at, w1)
    gather_plane(r, at, w2)
    halo(1, 5)
    make_state_grad(r, 1)
    gather_plane(r, at, v)
    halo(0, 4, 8)
    gather_core(r, at, w0)
    gather_core(r, at, w1)
    gather_end(r, at, w0)
    gather_end(r, at, w1)
    gather_core(r, at, w2)
    gather_end(r, at, w2)
    gather_core(r, at, v)
    gather_end(r, at, v)
    drain(r, at)


def move_kernel(*refs):
    sem = refs[-1]
    copies = [pltpu.make_async_copy(refs[i], refs[5 + i], sem.at[i]) for i in range(5)]
    for copy in copies:
        copy.start()
    for copy in copies:
        copy.wait()


def shards(states, pre_act, features, cotangent, halo_states, halo_cot, coupling, tile_blocks, tile_rows, tile_cols, tile_counts, send_rows, send_counts, recv_counts, w_state, w_input):
    far = pl.BlockSpec(memory_space=pl.ANY)
    smem = pl.BlockSpec(memory_space=pltpu.SMEM)
    vmem = pl.BlockSpec(memory_space=pltpu.VMEM)
    wide = jax.ShapeDtypeStruct((2048, 768), BF16)
    results = (
        wide,
        jax.ShapeDtypeStruct((2048, 256), BF16),
        jax.ShapeDtypeStruct((3, 256, 256), F32),
        jax.ShapeDtypeStruct((3, 256, 256), F32),
        jax.ShapeDtypeStruct((576, 768), BF16),
    )
    hbm = pl.BlockSpec(memory_space=pltpu.HBM)

    def stay(value):
        return pltpu.with_memory_space_constraint(value, pltpu.HBM)

    pg, tiles, meta = pl.pallas_call(
        first_kernel,
        out_shape=(wide, jax.ShapeDtypeStruct((65, 128, 128), BF16), jax.ShapeDtypeStruct((8, 128), jnp.int32)),
        in_specs=[smem] + [hbm] * 5,
        out_specs=(vmem,) * 3,
        scratch_shapes=list(FIRST_SCRATCH.values()),
        compiler_params=pltpu.CompilerParams(vmem_limit_bytes=FIRST_LIMIT * 2**20),
        name="first",
    )(tile_counts, *[stay(v) for v in (tile_rows, tile_cols, pre_act, cotangent, tile_blocks)])
    found = pl.pallas_call(
        rest_kernel,
        out_shape=results,
        in_specs=[smem] * 3 + [vmem] * 4 + [hbm] * 3 + [vmem, hbm, vmem, vmem],
        out_specs=(vmem,) * 5,
        scratch_shapes=list(REST_SCRATCH.values()) + [kind for group in GROUPS for kind in group_scratch(group[2]).values()],
        compiler_params=pltpu.CompilerParams(collective_id=0, has_side_effects=True, vmem_limit_bytes=REST_LIMIT * 2**20),
        name="rest",
    )(send_counts, recv_counts, meta, pg, pg.reshape(16, 128, 768), tiles, states, stay(features), stay(halo_states), stay(halo_cot), coupling.T, stay(send_rows), w_state, w_input)
    return pl.pallas_call(
        move_kernel,
        out_shape=results,
        in_specs=[vmem] * 5,
        out_specs=(far,) * 5,
        scratch_shapes=[pltpu.SemaphoreType.DMA((5,))],
        compiler_params=pltpu.CompilerParams(vmem_limit_bytes=2**20),
        name="move",
    )(*found)


FIRST_LIMIT = 14
REST_LIMIT = 32


def solution(mesh):
    rows = P("dom", None)
    one = P("dom")
    return jax.shard_map(
        shards,
        mesh=mesh,
        in_specs=(rows,) * 7 + (P("dom", None, None), one, one, one, rows, one, one, P(), P()),
        out_specs=(rows, rows, P(), P(), rows),
        check_vma=False,
    )
```

```python
from types import SimpleNamespace

import jax
import jax.numpy as jnp
from jax import lax
from jax.experimental import pallas as pl
from jax.experimental.pallas import tpu as pltpu
from jax.sharding import PartitionSpec as P

MESH = pl.DeviceIdType.MESH
F32 = jnp.float32
BF16 = jnp.bfloat16

OFFSETS = (1, 2, 3, 4, -1, -2, -3, -4, 64)
SLOTS = 9
CAP = 64
NT = (((1,), (1,)), ((), ()))
TN = (((0,), (0,)), ((), ()))


def dot(a, b):
    return jnp.dot(a, b, preferred_element_type=F32)


def dot_nt(a, b):
    return lax.dot_general(a, b, NT, preferred_element_type=F32)


def dot_tn(a, b):
    return lax.dot_general(a, b, TN, preferred_element_type=F32)


def order_tiles(r):
    r.load_tile_rows.wait()
    r.load_tile_cols.wait()
    count = r.tile_counts[0]
    sub = lax.broadcasted_iota(jnp.int32, (8, 128), 0)
    tile = lax.broadcasted_iota(jnp.int32, (64, 128), 0)
    lane = lax.broadcasted_iota(jnp.int32, (64, 128), 1)
    lane1 = lax.broadcasted_iota(jnp.int32, (1, 128), 1)
    zero = jnp.zeros((64, 128), jnp.int32)
    keys, rows = [], []
    for t in range(64):
        keys.append(jnp.where(t < count, r.s_tile_cols[t], 16))
        rows.append(r.s_tile_rows[t])

    def column(values):
        parts = []
        for b in range(8):
            part = jnp.zeros((8, 128), jnp.int32)
            for i in range(8):
                part = jnp.where(sub == i, values[8 * b + i], part)
            parts.append(part)
        return jnp.concatenate(parts, axis=0)

    key, row = column(keys), column(rows)
    place = zero
    for s in range(64):
        place += jnp.where((key == keys[s]) & (tile > s), 1, 0)
    base = zero
    upto = jnp.zeros((1, 128), jnp.int32)
    inside = jnp.zeros((1, 128), jnp.int32)
    for c in range(16):
        here = jnp.sum(jnp.where(key == c, 1, 0), axis=0, keepdims=True)
        pairs = (here + 1) >> 1
        base += jnp.where(key > c, pairs, 0)
        upto += jnp.where(lane1 >= c, pairs, 0)
        inside += jnp.where(lane1 == c, here, 0)
    at = jnp.where(key < 16, base + (place >> 1), 1000)
    first = (at == lane) & ((place & 1) == 0)
    second = (at == lane) & ((place & 1) == 1)

    def total(mask, value):
        return jnp.sum(jnp.where(mask, value, 0), axis=0, keepdims=True)

    meta = (total(first, tile - 64) + 64, total(second, tile - 64) + 64, total(first, row), total(second, row), total(first & (place > 0), 1), upto, jnp.minimum(inside, 1))
    for i, value in enumerate(meta):
        r.meta[i : i + 1, :] = value
    r.meta[7:8, :] = jnp.zeros((1, 128), jnp.int32)


def make_pre_grad(r):
    for i in range(4):
        r.load_acts[i].wait()
        r.load_cots[i].wait()

        @pl.loop(0, 4)
        def _(b):
            rows = pl.ds(pl.multiple_of(512 * i + 128 * b, 128), 128)
            third = (r.ct[rows, :].astype(F32) * (1.0 / 3.0)).astype(BF16)
            for k in range(3):
                cols = slice(256 * k, 256 * k + 256)
                act = r.pg[rows, cols]
                r.pg[rows, cols] = jnp.where(act > 0, third, jnp.zeros_like(third))


def make_one_hot(r):
    r.load_send_rows.wait()
    index = r.v_send_rows[...].T
    slot = lax.broadcasted_iota(jnp.int32, (CAP, 1), 0)
    node = lax.broadcasted_iota(jnp.int32, (CAP, 2048), 1)
    for j in range(SLOTS):
        mine = jnp.where(slot < r.send_counts[j], index[:, j : j + 1], -1)
        r.oh[CAP * j : CAP * j + CAP, :] = jnp.where(node == mine, 1.0, 0.0).astype(BF16)


def make_outgoing(r, k):
    cols = slice(256 * k, 256 * k + 256)
    r.outgoing[:, cols] = dot(r.oh[...], r.pg[:, cols]).astype(BF16)


def make_feature_grad(r):
    @pl.loop(0, 2)
    def _(b):
        rows = pl.ds(pl.multiple_of(1024 * b, 1024), 1024)
        total = dot_nt(r.pg[rows, 0:256], r.w_input[0])
        for k in (1, 2):
            total += dot_nt(r.pg[rows, 256 * k : 256 * k + 256], r.w_input[k])
        r.feature_grad[rows, :] = total.astype(BF16)


def make_v(r):
    r.load_features.wait()
    for b in range(2):
        rows = pl.ds(1024 * b, 1024)
        left = r.v_features[rows, :].T
        for k in range(3):
            part = dot(left, r.pg[rows, 256 * k : 256 * k + 256])
            r.gacc[0, k] = part if b == 0 else r.gacc[0, k] + part


def mask_halo(r, ref):
    slot = lax.broadcasted_iota(jnp.int32, (CAP, 768), 0)
    for j in range(SLOTS):
        rows = slice(CAP * j, CAP * j + CAP)
        ref[rows, :] = jnp.where(slot < r.recv_counts[j], ref[rows, :].astype(F32), 0.0).astype(BF16)


def flip_tiles(r):
    r.tiles[64] = jnp.zeros((128, 128), BF16)
    r.load_tile_blocks.wait()

    @pl.loop(0, 64, unroll=16)
    def _(t):
        r.tiles[t] = r.tiles[t].T


def make_q(r, k):
    cols = slice(256 * k, 256 * k + 256)
    meta, tiles = r.meta, r.tiles

    @pl.loop(0, 40, unroll=20)
    def _(t):
        left = jnp.concatenate([tiles[meta[0, t]], tiles[meta[1, t]]], axis=1)
        right = jnp.concatenate([r.blocked[meta[2, t], :, cols], r.blocked[meta[3, t], :, cols]], axis=0)
        r.stage[t + 1] = dot(left, right) + r.stage[t] * meta[4, t].astype(F32)

    @pl.loop(0, 16, unroll=8)
    def _(c):
        value = r.stage[meta[5, c]] * meta[6, c].astype(F32)
        r.qb[pl.ds(pl.multiple_of(c * 128, 128), 128), cols] = value.astype(BF16)


def make_w(r, k):
    cols = slice(256 * k, 256 * k + 256)
    meet = dot(r.coupling[...], r.pg[:, cols]).astype(BF16)
    r.gacc[1, k] = dot_tn(r.v_halo_states[:, cols], meet)
    for b in range(2):
        rows = pl.ds(1024 * b, 1024)
        r.gacc[1, k] += dot_tn(r.states[rows, cols], r.qb[rows, cols])


def make_e(r):
    r.load_halo_cot.wait()
    mask_halo(r, r.v_halo_cot)
    for k in range(3):
        cols = slice(256 * k, 256 * k + 256)
        r.ee[:, cols] = dot_nt(r.v_halo_cot[:, cols], r.w_state[k]).astype(BF16)


def make_state_grad(r, half):
    @pl.loop(0, 2)
    def _(b):
        rows = pl.ds(pl.multiple_of(1024 * half + 512 * b, 512), 512)
        left = r.coupling[:, rows].T
        for k in range(3):
            cols = slice(256 * k, 256 * k + 256)
            total = dot(left, r.ee[:, cols]) + dot_nt(r.qb[rows, cols], r.w_state[k])
            r.state_grad[rows, cols] = total.astype(BF16)


class Place:
    def __init__(self):
        self.me = lax.axis_index("dom")
        self.x = lax.div(self.me, 32)
        self.z = lax.rem(lax.div(self.me, 8), 4)
        self.y = lax.rem(lax.div(self.me, 2), 4)
        self.core = lax.rem(self.me, 2)
        self.own = self.x * 4 + self.z
        self.xs = [lax.rem(self.x + j, 4) for j in range(4)]
        self.zs = [lax.rem(self.z + j, 4) for j in range(4)]
        self.sibling = self.me + 1 - 2 * self.core
        low = self.y * 2 + self.core
        self.plane = []
        for n in FAR_FIRST:
            to = self.xs[n // 4] * 4 + self.zs[n % 4]
            self.plane.append((n, to, to * 8 + low))
        base = self.me - self.y * 2
        self.line = [base + 2 * lax.rem(self.y + j, 4) for j in (1, 2, 3)]
        self.halo = [lax.rem(self.me + 128 + offset, 128) for offset in OFFSETS]


FAR_FIRST = (10, 6, 14, 9, 11, 5, 7, 13, 15, 2, 8, 1, 3, 4, 12)


def remote(src, dst, send, recv, device):
    return pltpu.make_async_remote_copy(src_ref=src, dst_ref=dst, send_sem=send, recv_sem=recv, device_id=(device,), device_id_type=MESH)


def greet(at):
    barrier = pltpu.get_barrier_semaphore()
    for device in [at.sibling] + [device for _, _, device in at.plane] + at.line + at.halo:
        pl.semaphore_signal(barrier, inc=1, device_id=(device,), device_id_type=MESH)


def await_greetings():
    pl.semaphore_wait(pltpu.get_barrier_semaphore(), 1 + 15 + 3 + SLOTS)


def halo_copy(r, at, j):
    rows = pl.ds(CAP * j, CAP)
    return remote(r.outgoing.at[rows], r.sent_cot.at[rows], r.halo_send.at[j], r.halo_recv.at[j], at.halo[j])


def halo_start(r, at, j):
    if j == SLOTS - 1:
        halo_copy(r, at, j).start()
        return
    flip = 1 - 2 * at.core
    slot = j + at.core * (4 if j < 4 else -4)
    rows = pl.ds(pl.multiple_of(slot * CAP, CAP), CAP)
    device = lax.rem(at.me + 128 + flip * OFFSETS[j], 128)
    remote(r.outgoing.at[rows], r.sent_cot.at[rows], r.halo_send.at[slot], r.halo_recv.at[slot], device).start()


def core_copy(at, g):
    return remote(g.half, g.core, g.a_send, g.a_recv, at.sibling)


def scatter_all(at, g):
    return remote(g.r1, g.r1, g.b_send, g.b_recv, at.sibling)


def line_copy(at, g, j):
    mine = g.r2.at[at.y]
    return remote(mine, mine, g.c_send.at[j], g.c_recv.at[j], at.line[j])


def gather_all(at, g):
    every = g.fin.at[0, pl.ds(0, 15)]
    return remote(every, every, g.d_send, g.d_recv, at.sibling)


def sibling_copy(at, g):
    mine = g.fin.at[at.core]
    return remote(mine, mine, g.e_send, g.e_recv, at.sibling)


def reduce_core(r, at, g):
    theirs = pl.ds(pl.multiple_of((1 - at.core) * 128, 128), 128)
    for i in range(g.count):
        g.half[i] = r.gacc[g.p, g.k + i, :, theirs].astype(BF16)
    core_copy(at, g).start()


def reduce_plane(r, at, g):
    ours = pl.ds(pl.multiple_of(at.core * 128, 128), 128)
    core_copy(at, g).wait_recv()
    for i in range(g.count):
        total = r.gacc[g.p, g.k + i, :, ours] + g.core[i].astype(F32)
        g.sum[i] = total
        g.send[:, i] = total.reshape(16, 16, 128).astype(BF16)
    for n, to, device in at.plane:
        remote(g.send.at[to], g.r1.at[n - 1], g.b_send, g.b_recv, device).start()


def reduce_line(r, at, g):
    rows = pl.ds(pl.multiple_of(at.own * 16, 16), 16)
    total = g.sum[:, rows, :]
    scatter_all(at, g).wait_recv()
    for n in range(15):
        total += g.r1[n].astype(F32)
    g.r2[at.y] = total
    for j in range(3):
        line_copy(at, g, j).start()


def gather_plane(r, at, g):
    for j in range(3):
        line_copy(at, g, j).wait_recv()
    total = (g.r2[0] + g.r2[1]) + (g.r2[2] + g.r2[3])
    g.fin[at.core, at.own] = total.astype(BF16)
    mine = g.fin.at[at.core, at.own]
    for _, _, device in at.plane:
        remote(mine, mine, g.d_send, g.d_recv, device).start()


def gather_core(r, at, g):
    gather_all(at, g).wait_recv()
    sibling_copy(at, g).start()


def gather_end(r, at, g):
    out = r.weight_grad if g.p else r.input_grad
    sibling_copy(at, g).wait_recv()
    for i in range(g.count):
        for c in range(2):
            block = g.fin[c, :, i].astype(F32).reshape(256, 128)
            out[g.k + i, :, 128 * c : 128 * c + 128] = block * (1.0 / 512.0)


def drain(r, at):
    for g in r.groups:
        core_copy(at, g).wait_send()
        scatter_all(at, g).wait_send()
        for j in range(3):
            line_copy(at, g, j).wait_send()
        gather_all(at, g).wait_send()
        sibling_copy(at, g).wait_send()
    for j in range(SLOTS):
        halo_copy(r, at, j).wait()


GROUPS = ((0, 0, 3), (1, 0, 1), (1, 1, 1), (1, 2, 1))
DMA = pltpu.SemaphoreType.DMA


def group_scratch(count):
    one = DMA(())
    return dict(
        half=pltpu.VMEM((count, 256, 128), BF16),
        core=pltpu.VMEM((count, 256, 128), BF16),
        sum=pltpu.VMEM((count, 256, 128), F32),
        send=pltpu.VMEM((16, count, 16, 128), BF16),
        r1=pltpu.VMEM((15, count, 16, 128), BF16),
        r2=pltpu.VMEM((4, count, 16, 128), F32),
        fin=pltpu.VMEM((2, 16, count, 16, 128), BF16),
        a_send=one, a_recv=one, b_send=one, b_recv=one, c_send=DMA((3,)), c_recv=DMA((3,)),
        d_send=one, d_recv=one, e_send=one, e_recv=one,
    )


FIRST_SCRATCH = dict(
    ct=pltpu.VMEM((2048, 256), BF16),
    s_tile_rows=pltpu.SMEM((64,), jnp.int32),
    s_tile_cols=pltpu.SMEM((64,), jnp.int32),
    in_sem=DMA((11,)),
)


def first_kernel(tile_counts, tile_rows, tile_cols, pre_act, cotangent, tile_blocks, pg, tiles, meta, *scratch):
    r = SimpleNamespace(**dict(zip(FIRST_SCRATCH, scratch, strict=True)), tile_counts=tile_counts, pg=pg, tiles=tiles, meta=meta)

    def load(i, src, dst):
        copy = pltpu.make_async_copy(src, dst, r.in_sem.at[i])
        copy.start()
        return copy

    r.load_tile_rows = load(0, tile_rows, r.s_tile_rows)
    r.load_tile_cols = load(1, tile_cols, r.s_tile_cols)
    parts = [pl.ds(512 * i, 512) for i in range(4)]
    r.load_cots, r.load_acts = [], []
    for i, rows in enumerate(parts):
        r.load_cots.append(load(2 + i, cotangent.at[rows], r.ct.at[rows]))
        r.load_acts.append(load(6 + i, pre_act.at[rows], pg.at[rows]))
    r.load_tile_blocks = load(10, tile_blocks, tiles.at[pl.ds(0, 64)])
    order_tiles(r)
    make_pre_grad(r)
    flip_tiles(r)


REST_SCRATCH = dict(
    stage=pltpu.VMEM((41, 128, 256), F32),
    qb=pltpu.VMEM((2048, 768), BF16),
    v_send_rows=pltpu.VMEM((9, 64), jnp.int32),
    v_features=pltpu.VMEM((2048, 256), BF16),
    v_halo_states=pltpu.VMEM((576, 768), BF16),
    v_halo_cot=pltpu.VMEM((576, 768), BF16),
    oh=pltpu.VMEM((576, 2048), BF16),
    ee=pltpu.VMEM((576, 768), BF16),
    outgoing=pltpu.VMEM((576, 768), BF16),
    gacc=pltpu.VMEM((2, 3, 256, 256), F32),
    in_sem=DMA((4,)),
    halo_send=DMA((9,)),
    halo_recv=DMA((9,)),
)


def rest_refs(send_counts, recv_counts, meta, pg, blocked, tiles, states, features, halo_states, halo_cot, coupling, send_rows, w_state, w_input, state_grad, feature_grad, weight_grad, input_grad, sent_cot, *scratch):
    scratch = list(scratch)
    own = dict(zip(REST_SCRATCH, scratch))
    del scratch[: len(own)]
    r = SimpleNamespace(**own, send_counts=send_counts, recv_counts=recv_counts, meta=meta, pg=pg, blocked=blocked, tiles=tiles, states=states, coupling=coupling, w_state=w_state, w_input=w_input)
    r.state_grad, r.feature_grad, r.weight_grad, r.input_grad, r.sent_cot = state_grad, feature_grad, weight_grad, input_grad, sent_cot
    r.groups = []
    for p, k, count in GROUPS:
        kinds = group_scratch(count)
        r.groups.append(SimpleNamespace(**dict(zip(kinds, scratch)), p=p, k=k, count=count))
        del scratch[: len(kinds)]

    def load(i, src, dst):
        copy = pltpu.make_async_copy(src, dst, r.in_sem.at[i])
        copy.start()
        return copy

    r.load_halo_states = load(0, halo_states, r.v_halo_states)
    r.load_features = load(1, features, r.v_features)
    r.load_send_rows = load(2, send_rows, r.v_send_rows)
    r.load_halo_cot = load(3, halo_cot, r.v_halo_cot)
    return r


def rest_kernel(*refs):
    r = rest_refs(*refs)
    v, w0, w1, w2 = r.groups
    at = Place()
    greet(at)

    def halo(*slots):
        for j in slots:
            halo_start(r, at, j)

    r.stage[0] = jnp.zeros((128, 256), F32)
    make_q(r, 0)
    r.load_halo_states.wait()
    mask_halo(r, r.v_halo_states)
    make_w(r, 0)
    await_greetings()
    reduce_core(r, at, w0)
    make_v(r)
    reduce_core(r, at, v)
    reduce_plane(r, at, w0)
    make_one_hot(r)
    make_outgoing(r, 0)
    reduce_plane(r, at, v)
    make_outgoing(r, 1)
    make_outgoing(r, 2)
    halo(3, 7, 8)
    make_q(r, 1)
    make_w(r, 1)
    reduce_core(r, at, w1)
    reduce_line(r, at, w0)
    reduce_line(r, at, v)
    halo(2, 6)
    make_q(r, 2)
    reduce_plane(r, at, w1)
    make_w(r, 2)
    reduce_core(r, at, w2)
    gather_plane(r, at, w0)
    gather_plane(r, at, v)
    make_e(r)
    reduce_plane(r, at, w2)
    halo(1, 5, 0, 4)
    make_feature_grad(r)
    reduce_line(r, at, w1)
    make_state_grad(r, 0)
    reduce_line(r, at, w2)
    gather_core(r, at, w0)
    gather_core(r, at, v)
    gather_plane(r, at, w1)
    make_state_grad(r, 1)
    gather_plane(r, at, w2)
    gather_end(r, at, w0)
    gather_end(r, at, v)
    gather_core(r, at, w1)
    gather_end(r, at, w1)
    gather_core(r, at, w2)
    gather_end(r, at, w2)
    drain(r, at)


def move_kernel(*refs):
    sem = refs[-1]
    copies = [pltpu.make_async_copy(refs[i], refs[5 + i], sem.at[i]) for i in range(5)]
    for copy in copies:
        copy.start()
    for copy in copies:
        copy.wait()


def shards(states, pre_act, features, cotangent, halo_states, halo_cot, coupling, tile_blocks, tile_rows, tile_cols, tile_counts, send_rows, send_counts, recv_counts, w_state, w_input):
    far = pl.BlockSpec(memory_space=pl.ANY)
    smem = pl.BlockSpec(memory_space=pltpu.SMEM)
    vmem = pl.BlockSpec(memory_space=pltpu.VMEM)
    wide = jax.ShapeDtypeStruct((2048, 768), BF16)
    results = (
        wide,
        jax.ShapeDtypeStruct((2048, 256), BF16),
        jax.ShapeDtypeStruct((3, 256, 256), F32),
        jax.ShapeDtypeStruct((3, 256, 256), F32),
        jax.ShapeDtypeStruct((576, 768), BF16),
    )
    hbm = pl.BlockSpec(memory_space=pltpu.HBM)

    def stay(value):
        return pltpu.with_memory_space_constraint(value, pltpu.HBM)

    pg, tiles, meta = pl.pallas_call(
        first_kernel,
        out_shape=(wide, jax.ShapeDtypeStruct((65, 128, 128), BF16), jax.ShapeDtypeStruct((8, 128), jnp.int32)),
        in_specs=[smem] + [hbm] * 5,
        out_specs=(vmem,) * 3,
        scratch_shapes=list(FIRST_SCRATCH.values()),
        compiler_params=pltpu.CompilerParams(vmem_limit_bytes=FIRST_LIMIT * 2**20),
        name="first",
    )(tile_counts, *[stay(v) for v in (tile_rows, tile_cols, pre_act, cotangent, tile_blocks)])
    found = pl.pallas_call(
        rest_kernel,
        out_shape=results,
        in_specs=[smem] * 3 + [vmem] * 4 + [hbm] * 3 + [vmem, hbm, vmem, vmem],
        out_specs=(vmem,) * 5,
        scratch_shapes=list(REST_SCRATCH.values()) + [kind for group in GROUPS for kind in group_scratch(group[2]).values()],
        compiler_params=pltpu.CompilerParams(collective_id=0, has_side_effects=True, vmem_limit_bytes=REST_LIMIT * 2**20),
        name="rest",
    )(send_counts, recv_counts, meta, pg, pg.reshape(16, 128, 768), tiles, states, stay(features), stay(halo_states), stay(halo_cot), coupling.T, stay(send_rows), w_state, w_input)
    return pl.pallas_call(
        move_kernel,
        out_shape=results,
        in_specs=[vmem] * 5,
        out_specs=(far,) * 5,
        scratch_shapes=[pltpu.SemaphoreType.DMA((5,))],
        compiler_params=pltpu.CompilerParams(vmem_limit_bytes=2**20),
        name="move",
    )(*found)


FIRST_LIMIT = 14
REST_LIMIT = 32


def solution(mesh):
    rows = P("dom", None)
    one = P("dom")
    return jax.shard_map(
        shards,
        mesh=mesh,
        in_specs=(rows,) * 7 + (P("dom", None, None), one, one, one, rows, one, one, P(), P()),
        out_specs=(rows, rows, P(), P(), rows),
        check_vma=False,
    )
```
